256 devices in a mesh: lon: 16 (over y_hi, z), lev: 4 (over x), lat: 4 (over y_lo, core).
Axes of the slice: x: 4, y: 4 (y_hi: 2, y_lo: 2; y = y_hi * 2 + y_lo), z: 8, core: 2. Of those that a mesh axis runs over, the one named last changes fastest.
Arguments:
- tokens: bfloat16 [2, 8, 48, 192, 192], P(None, 'lev', 'lat', 'lon'), may hold values from -40 to 40
- cotangent: bfloat16 [2, 8, 48, 192, 192], P(None, 'lev', 'lat', 'lon'), may hold values from -6 to 6
- w_qkv: bfloat16 [192, 576], replicated, may hold values from -0.4375 to 0.4375
- w_proj: bfloat16 [192, 192], replicated, may hold values from -0.4375 to 0.4375
- ln_gain: float32 [192], replicated, may hold values from 0.1 to 1.9
- ln_shift: float32 [192], replicated, may hold values from -3 to 3
- bias_table: float32 [32, 6, 3312], P(('lev', 'lat')), may hold values from -4 to 302
- region_ids: int32 [8, 48], P('lev', 'lat'), may hold values from 0 to 3
- lat_keep: int32 [48], P('lat'), may hold values 0 or 1
Outputs:
- grad_tokens: bfloat16 [2, 8, 48, 192, 192], P(None, 'lev', 'lat', 'lon')
- grad_qkv: float32 [192, 576], replicated
- grad_proj: float32 [192, 192], replicated
- grad_gain: float32 [192], replicated
- grad_shift: float32 [192], replicated
- grad_bias: float32 [32, 6, 3312], P(('lev', 'lat'), None, 'lon')
The draws below stay inside these ranges and needn't reach their ends.
All inputs are finite; a program needn't handle non-finite values. No bound on the sum of `lat_keep` on one device may be relied on, other than what follows from the above.
Results may differ from the reference program's by a relative error of at most 0.023.
Values may be sent and summed in bfloat16 or wider, within the bound.
A program may use at most 128 MiB of HBM per device.

```python
import math
import jax
import jax.numpy as jnp
from jax import lax

C = 192
HEADS = 6
WZ = 2
WH = 6
WW = 12
MEMBERS = 2
LEV = 8
LAT = 48
LON = 192
TYPES = 32


def draw_tokens(key, part):
    key = jax.random.fold_in(key, 11)
    key_base, key_rows, key_cols = jax.random.split(key, 3)
    shape = (MEMBERS, LEV, LAT, LON, C)
    row_scale = jnp.exp(jax.random.uniform(key_rows, (MEMBERS, LEV, LAT, LON, 1), jnp.float32, -1.15, 1.15))
    col_scale = jnp.exp(jax.random.uniform(key_cols, (C,), jnp.float32, -1.15, 1.15))
    base = jax.random.truncated_normal(key_base, -4.0, 4.0, shape, jnp.float32)
    return (base * row_scale * col_scale).astype(jnp.bfloat16)


def draw_bias_table(key, part):
    key = jax.random.fold_in(key, 23)
    key_base = jax.random.fold_in(key, 0)
    pairs = WZ * WZ * WH * WH
    span = 2 * WW - 1
    shape = (TYPES, HEADS, pairs, span)
    table = jax.random.truncated_normal(key_base, -4.0, 4.0, shape, jnp.float32)
    return table.reshape(TYPES, HEADS, pairs * span)


def with_ends(values, own_key, low, high):
    longest = values.shape.index(max(values.shape))
    spots = []
    for shift in (0, 1):
        where = [jax.random.randint(jax.random.fold_in(own_key, axis), (), 0, length) for axis, length in enumerate(values.shape)]
        where[longest] = (where[longest] + shift) % values.shape[longest]
        spots.append(tuple(where))
    return values.at[spots[0]].set(low).at[spots[1]].set(high)


def block_levels(key, dims, cuts, smallest, largest):
    loudness, own = 1.0, jax.random.fold_in(key, 6)
    for axis_at, blocks in cuts:
        heights = jnp.exp(jax.random.uniform(jax.random.fold_in(own, axis_at), (blocks,), jnp.float32, smallest / len(cuts), largest / len(cuts)))
        loudness = loudness * jnp.repeat(heights, dims[axis_at] // blocks).reshape([-1 if axis == axis_at else 1 for axis in range(len(dims))])
    return loudness


def gaussian(key, extent, width, bound, cuts=(), held_as=jnp.bfloat16):
    drawn = jax.random.normal(key, extent, jnp.float32) * width
    if len(cuts) > 0:
        drawn = block_levels(key, extent, cuts, -0.22, 0.18) * drawn
    return jnp.clip(drawn, min=-bound, max=bound).astype(held_as)


def setup_inputs(seed: int = 0) -> dict:
    key_of = jax.random.split(jax.random.key(seed), 10)
    return {
        "tokens": draw_tokens(jax.random.fold_in(key_of[9], 71), 0),
        "cotangent": gaussian(key_of[1], (MEMBERS, LEV, LAT, LON, C), 1.0, 6.0, ((1, 4), (2, 4), (3, 16))),
        "w_qkv": gaussian(key_of[2], (C, 3 * C), C ** -0.5, 0.4375),
        "w_proj": gaussian(key_of[3], (C, C), C ** -0.5, 0.4375),
        "ln_gain": jnp.clip(1.0 + 0.18 * jax.random.normal(key_of[4], (C,), jnp.float32), 0.1, 1.9),
        "ln_shift": gaussian(key_of[5], (C,), 0.5, 3.0, (), jnp.float32),
        "bias_table": draw_bias_table(jax.random.fold_in(key_of[9], 71), 0),
        "region_ids": with_ends(jax.random.randint(key_of[7], (LEV, LAT), 0, 4), jax.random.fold_in(key_of[7], 1), 0, 3).astype(jnp.int32),
        "lat_keep": with_ends((jax.random.randint(key_of[8], (LAT,), 0, 8) < 7).astype(jnp.int32), jax.random.fold_in(key_of[8], 1), 0, 1),
    }


ln_eps = 1e-05
masked_score = -1000000000.0

def offset_table():
    span = 2 * WW - 1
    offs = jnp.arange(span)[:, None, None]
    left = jnp.arange(WW)[None, :, None]
    right = jnp.arange(WW)[None, None, :]
    return (left - right + WW - 1 == offs).astype(jnp.float32)

def expand_table(rel_table):
    groups = rel_table.shape[0]
    seven = rel_table.reshape(groups, HEADS, WZ, WZ, WH, WH, 2 * WW - 1)
    full_bias = jnp.einsum('ghabcdr,rxy->ghacxbdy', seven, offset_table(), precision=lax.Precision.HIGHEST)
    return full_bias.reshape(groups, HEADS, WZ * WH * WW, WZ * WH * WW)

def fold_table(full_grad):
    groups = full_grad.shape[0]
    eight = full_grad.reshape(groups, HEADS, WZ, WH, WW, WZ, WH, WW)
    folded = jnp.einsum('ghacxbdy,rxy->ghabcdr', eight, offset_table(), precision=lax.Precision.HIGHEST)
    return folded.reshape(groups, HEADS, WZ * WZ * WH * WH * (2 * WW - 1))

def window_grad(token_win, grad_win, rel_table, same_region, w_qkv, w_proj, ln_gain, ln_shift):
    groups, win_count, win_tokens, channels = token_win.shape
    head_size = channels // HEADS
    row_count = groups * win_count * win_tokens
    rows_f = token_win.reshape(row_count, channels).astype(jnp.float32)
    row_mean = lax.optimization_barrier(jnp.mean(rows_f, -1, keepdims=True))
    centred = rows_f - row_mean
    inv_std = lax.rsqrt(lax.optimization_barrier(jnp.mean(centred * centred, -1, keepdims=True)) + ln_eps)
    x_hat = centred * inv_std
    normed = (x_hat * ln_gain + ln_shift).astype(jnp.bfloat16)
    qkv = jnp.dot(normed, w_qkv, preferred_element_type=jnp.float32).astype(jnp.bfloat16)
    head_split = qkv.reshape(groups, win_count, win_tokens, 3, HEADS, head_size)
    queries = head_split[:, :, :, 0].astype(jnp.float32)
    key_rows = head_split[:, :, :, 1].astype(jnp.float32)
    values = head_split[:, :, :, 2].astype(jnp.float32)
    score_scale = head_size ** (-0.5)
    scores = jnp.einsum('gwihd,gwjhd->gwhij', queries, key_rows) * score_scale
    scores = scores + expand_table(rel_table)[:, None]
    scores = jnp.where(same_region[:, None, None], scores, masked_score)
    row_max = lax.optimization_barrier(jnp.max(scores, -1, keepdims=True))
    exp_scores = jnp.exp(scores - row_max)
    attn_probs = exp_scores / lax.optimization_barrier(jnp.sum(exp_scores, -1, keepdims=True))
    probs_b = attn_probs.astype(jnp.bfloat16).astype(jnp.float32)
    attended = jnp.einsum('gwhij,gwjhd->gwihd', probs_b, values).astype(jnp.bfloat16).reshape(row_count, channels)
    grad_rows = grad_win.reshape(row_count, channels)
    d_wproj = jnp.dot(attended.T, grad_rows, preferred_element_type=jnp.float32)
    d_attended = jnp.dot(grad_rows, w_proj.T, preferred_element_type=jnp.float32).astype(jnp.bfloat16)
    d_attended = d_attended.reshape(groups, win_count, win_tokens, HEADS, head_size).astype(jnp.float32)
    d_probs = jnp.einsum('gwihd,gwjhd->gwhij', d_attended, values)
    d_values = jnp.einsum('gwhij,gwihd->gwjhd', probs_b, d_attended).astype(jnp.bfloat16)
    d_scores = attn_probs * (d_probs - lax.optimization_barrier(jnp.sum(attn_probs * d_probs, -1, keepdims=True)))
    d_table = fold_table(lax.optimization_barrier(jnp.sum(d_scores, 1)))
    scaled = (d_scores * score_scale).astype(jnp.bfloat16).astype(jnp.float32)
    d_queries = jnp.einsum('gwhij,gwjhd->gwihd', scaled, key_rows).astype(jnp.bfloat16)
    d_keys = jnp.einsum('gwhij,gwihd->gwjhd', scaled, queries).astype(jnp.bfloat16)
    d_qkv = jnp.stack([d_queries, d_keys, d_values], axis=3).reshape(row_count, 3 * channels)
    d_wqkv = jnp.dot(normed.T, d_qkv, preferred_element_type=jnp.float32)
    d_normed = jnp.dot(d_qkv, w_qkv.T, preferred_element_type=jnp.float32)
    d_gain = lax.optimization_barrier(jnp.sum(d_normed * x_hat, 0))
    d_shift = lax.optimization_barrier(jnp.sum(d_normed, 0))
    d_hat = d_normed * ln_gain
    d_rows = inv_std * (d_hat - lax.optimization_barrier(jnp.mean(d_hat, -1, keepdims=True)) - x_hat * lax.optimization_barrier(jnp.mean(d_hat * x_hat, -1, keepdims=True)))
    d_rows = d_rows.astype(jnp.bfloat16).reshape(groups, win_count, win_tokens, channels)
    return (d_rows, d_table, d_wqkv, d_wproj, d_gain, d_shift)

def partition(field):
    members, levels, rows, longs, channels = field.shape
    split = field.reshape(members, levels // WZ, WZ, rows // WH, WH, longs // WW, WW, channels)
    split = split.transpose(1, 3, 0, 5, 2, 4, 6, 7)
    return split.reshape(levels // WZ * (rows // WH), members * (longs // WW), WZ * WH * WW, channels)

def assemble(windows, members, levels, rows, longs):
    channels = windows.shape[-1]
    split = windows.reshape(levels // WZ, rows // WH, members, longs // WW, WZ, WH, WW, channels)
    split = split.transpose(2, 0, 4, 1, 5, 3, 6, 7)
    return split.reshape(members, levels, rows, longs, channels)

def region_windows(region_ids):
    levels, rows = region_ids.shape
    split = region_ids.reshape(levels // WZ, WZ, rows // WH, WH).transpose(0, 2, 1, 3)
    split = split.reshape(levels // WZ * (rows // WH), WZ * WH)
    per_token = jnp.repeat(split, WW, axis=1)
    return per_token[:, :, None] == per_token[:, None, :]

def reference(tokens, cotangent, w_qkv, w_proj, ln_gain, ln_shift, bias_table, region_ids, lat_keep):
    masked = cotangent * lat_keep[None, None, :, None, None].astype(jnp.bfloat16)
    offsets_fwd = (-(WZ // 2), -(WH // 2), -(WW // 2))
    shifted_tokens = jnp.roll(tokens, offsets_fwd, (1, 2, 3))
    shifted_grad = jnp.roll(masked, offsets_fwd, (1, 2, 3))
    token_windows = partition(shifted_tokens)
    grad_windows = partition(shifted_grad)
    same_region = region_windows(region_ids)
    channels = tokens.shape[-1]

    def block_step(sums, item):
        token_win, grad_win, rel_table, same_block = item
        d_rows, d_table, d_wqkv, d_wproj, d_gain, d_shift = window_grad(token_win[None], grad_win[None], rel_table[None], same_block[None], w_qkv, w_proj, ln_gain, ln_shift)
        sums = (sums[0] + d_wqkv, sums[1] + d_wproj, sums[2] + d_gain, sums[3] + d_shift)
        return (sums, (d_rows[0], d_table[0]))
    start = (jnp.zeros((channels, 3 * channels), jnp.float32), jnp.zeros((channels, channels), jnp.float32), jnp.zeros((channels,), jnp.float32), jnp.zeros((channels,), jnp.float32))
    sums, (d_windows, d_tables) = lax.scan(block_step, start, (token_windows, grad_windows, bias_table, same_region))
    d_shifted = assemble(d_windows, MEMBERS, LEV, LAT, LON)
    back = jnp.roll(d_shifted, (WZ // 2, WH // 2, WW // 2), (1, 2, 3))
    grad_tokens = (cotangent.astype(jnp.float32) + back.astype(jnp.float32)).astype(jnp.bfloat16)
    grad_scale = 1.0 / math.sqrt(MEMBERS * LEV * LAT * LON)
    return (grad_tokens, sums[0] * grad_scale, sums[1] * grad_scale, sums[2] * grad_scale, sums[3] * grad_scale, d_tables)
```

```python
import math

import jax
import jax.numpy as jnp
import numpy as np
from jax import lax
from jax.experimental import pallas as pl
from jax.experimental.pallas import tpu as pltpu
from jax.sharding import PartitionSpec as P

MESH = pl.DeviceIdType.MESH
F32 = jnp.float32
BF16 = jnp.bfloat16

HEADS = 6
WZ = 2
WH = 6
WW = 12
MEMBERS = 2
LEVELS = 2
ROWS = 12
LONGS = 12
C = 192
DH = C // HEADS
WIN = WZ * WH * WW
TYPES = 2
TOKENS = MEMBERS * LEVELS * ROWS * LONGS
SPAN = 2 * WW - 1
FOLD = WH * SPAN
PIECES = 640
MASKED = -1000000000.0
EPS = 1e-05

PIECE_AT = [0, 112, 224, 336, 448, 496, 544, 592]
PIECE_LEN = [112, 112, 112, 112, 48, 48, 48, 48]
BLOCKS = 13


def piece_steps(q):
    return (q // 2) % 2, q // 4, q % 2


def index_rows():
    out = np.full((16, PIECES), -1, np.int32)
    of_natural = np.full(PIECES, -1, np.int32)
    of_window = np.full(PIECES, -1, np.int32)
    for q in range(8):
        dz, dh, dw = piece_steps(q)
        rows = 3 if dh else 9
        for m in range(MEMBERS):
            for hh in range(rows):
                for ww in range(6):
                    s = PIECE_AT[q] + (m * rows + hh) * 6 + ww
                    lev = 1 - dz
                    row = hh if dh else 3 + hh
                    lon = ww if dw else 6 + ww
                    of_natural[s] = ((m * LEVELS + lev) * ROWS + row) * LONGS + lon
                    there = 9 + hh if dh else hh
                    t, h = there // WH, there % WH
                    w = 6 + ww if dw else ww
                    of_window[s] = (t * MEMBERS + m) * WIN + w * 12 + dz * WH + h
    out[0] = of_natural
    out[3] = of_window
    for s in range(PIECES):
        if of_natural[s] >= 0:
            out[2, of_natural[s]] = s
            out[1, of_window[s]] = s
    for rr in range(SPAN):
        for zj in range(WZ):
            for hj in range(WH):
                out[4, (rr * WZ + zj) * WH + hj] = zj * 256 + hj * SPAN + SPAN - 1 - rr
    for b in range(12):
        for t in range(TYPES):
            for h in range(HEADS):
                th, slot = t * HEADS + h, t * 8 + h
                out[5, b * 16 + slot] = th * 16 + b
                out[6, th * 16 + b] = b * 16 + slot
    for zj in range(WZ):
        for hj in range(WH):
            for r in range(SPAN):
                src = ((SPAN - 1 - r) * WZ + zj) * WH + hj
                flat = hj * SPAN + r
                out[7 + zj, flat] = src
                if hj < 3:
                    out[9 + zj, FOLD + flat] = src
                else:
                    out[11 + zj, flat - FOLD // 2] = src
                out[13 + zj, FOLD // 2 + flat] = src
    out[15, :384] = np.arange(384) % 12
    return out


def dot(a, b):
    return lax.dot_general(a, b, (((1,), (0,)), ((), ())), preferred_element_type=F32)


def dot_nt(a, b):
    return lax.dot_general(a, b, (((1,), (1,)), ((), ())), preferred_element_type=F32)


def dot_tn(a, b):
    return lax.dot_general(a, b, (((0,), (0,)), ((), ())), preferred_element_type=F32)


def make_body(lon_n, lev_n, lat_n):
    z_n = lon_n // 2
    y_n = lat_n // 2
    plane_n = 2 * y_n * lev_n
    total = MEMBERS * LEVELS * ROWS * LONGS * lon_n * lev_n * lat_n
    grad_scale = 1.0 / math.sqrt(total)
    score_scale = DH ** (-0.5)

    def body(
        tok, cot, wqkv, wproj, gain, shift, table, reg, keep, idx,
        out_tok, out_qkv, out_proj, out_gain, out_shift, out_bias,
        ztok, zcot, sbuf, rbuf, xt, xg, dx, sb2, rb2,
        xk, bm, dacc, w3, wt, pw, pwt, pnt, qkvt, dqt, ot,
        accq, accp, accs, payf, payb, pairb, rsrc, plb, zbuf, fbuf, bmsg, brcv,
        s_h, r_h, s_o, r_o, s_p, r_p, s_1, r_1, s_2, r_2, s_3, r_3, s_4, r_4, s_b, r_b,
    ):
        o = lax.axis_index("lon")
        lv = lax.axis_index("lev")
        la = lax.axis_index("lat")
        core = lax.rem(la, 2)
        ylo = lax.div(la, 2)
        zz = lax.rem(o, z_n)
        yhi = lax.div(o, z_n)
        me_p = (yhi * y_n + ylo) * lev_n + lv

        def halo_dev(q, sign):
            dz, dh, dw = piece_steps(q)
            return {
                "lon": lax.rem(o + sign * dw + lon_n, lon_n),
                "lev": lax.rem(lv + sign * dz + lev_n, lev_n),
                "lat": lax.rem(la + sign * dh + lat_n, lat_n),
            }

        def plane_dev(p):
            ph = lax.div(p, y_n * lev_n)
            rest = lax.rem(p, y_n * lev_n)
            return {
                "lon": ph * z_n + zz,
                "lev": lax.rem(rest, lev_n),
                "lat": lax.div(rest, lev_n) * 2 + core,
            }

        def z_dev(k):
            return {"lon": yhi * z_n + lax.rem(zz + k, z_n), "lev": lv, "lat": la}

        def lon_dev(k):
            return {"lon": lax.rem(o + k, lon_n), "lev": lv, "lat": la}

        pair_dev = {"lon": o, "lev": lv, "lat": ylo * 2 + 1 - core}

        def remote(src, dst, ssem, rsem, dev):
            return pltpu.make_async_remote_copy(
                src_ref=src, dst_ref=dst, send_sem=ssem, recv_sem=rsem,
                device_id=dev, device_id_type=MESH,
            )

        partners = [halo_dev(q, s) for q in range(1, 8) for s in (-1, 1)]
        partners.append(pair_dev)
        partners += [plane_dev(lax.rem(me_p + k, plane_n)) for k in range(1, plane_n)]
        partners += [lon_dev(k) for k in range(1, lon_n)]
        barrier = pltpu.get_barrier_semaphore()
        for dev in partners:
            pl.semaphore_signal(barrier, inc=1, device_id=dev, device_id_type=MESH)

        def onehot(row, height, width):
            pick = lax.broadcasted_iota(jnp.int32, (height, width), 0) == idx[row : row + 1, 0:width]
            return jnp.where(pick, 1.0, 0.0).astype(BF16)

        for k in range(TOKENS // 24):
            for half in range(2):
                slab = 2 * k + half
                at = 24 * k + 12 * half
                ztok[at : at + 12, :] = tok[slab].astype(F32)
                kept = keep[0, slab % ROWS].astype(F32)
                zcot[at : at + 12, :] = cot[slab].astype(F32) * kept
        gather = onehot(2, PIECES, TOKENS)
        piece_tok = dot(gather, ztok[...].astype(BF16))
        piece_cot = dot(gather, zcot[...].astype(BF16))
        sbuf[...] = jnp.concatenate([piece_tok, piece_cot], axis=1).astype(BF16)

        pl.semaphore_wait(barrier, len(partners))
        halo = []
        for q in range(1, 8):
            part = pl.ds(PIECE_AT[q], PIECE_LEN[q])
            copy = remote(sbuf.at[part], rbuf.at[part], s_h.at[q], r_h.at[q], halo_dev(q, -1))
            copy.start()
            halo.append(copy)
        rbuf[0:112, :] = sbuf[0:112, :]

        dacc[...] = jnp.zeros_like(dacc)
        accq[...] = jnp.zeros_like(accq)
        accp[...] = jnp.zeros_like(accp)
        accs[...] = jnp.zeros_like(accs)
        xk[...] = jnp.zeros_like(xk)
        for zi in range(WZ):
            for zj in range(WZ):
                for hi in range(WH):
                    kappa = (zi * WZ + zj) * WH + hi
                    b = zi * WH + hi
                    for t in range(TYPES):
                        xk[b * 16 + t * 8 : b * 16 + t * 8 + 6, zj * 256 : zj * 256 + FOLD] = table[
                            t, :, kappa * FOLD : (kappa + 1) * FOLD
                        ]
        to_th = onehot(5, 192, 192)
        to_lane = onehot(4, 512, 384)
        rest = xk[...]
        wide = jnp.zeros((192, 384), F32)
        for _ in range(3):
            term = rest.astype(BF16)
            rest = rest - term.astype(F32)
            wide = wide + dot(dot(to_th, term).astype(BF16), to_lane)
        lane_a = idx[15:16, 0:384]
        row_b = lax.broadcasted_iota(jnp.int32, (16, 384), 0)
        masked = []
        for t in range(TYPES):
            reg_a = jnp.zeros((16, 384), jnp.int32)
            reg_b = jnp.zeros((16, 384), jnp.int32)
            for z in range(WZ):
                for h in range(WH):
                    ident = reg[z, t * WH + h]
                    reg_a = jnp.where(lane_a == z * WH + h, ident, reg_a)
                    reg_b = jnp.where(row_b == z * WH + h, ident, reg_b)
            for h in range(HEADS):
                th = t * HEADS + h
                masked.append(jnp.where(reg_a == reg_b, wide[th * 16 : th * 16 + 16], MASKED))
        wide = jnp.concatenate(masked, axis=0)
        for x in range(WW):
            moved = pltpu.roll(wide, (384 - 12 * (WW - 1 - x)) % 384, 1) if x < WW - 1 else wide
            for th in range(TYPES * HEADS):
                bm[th, 12 * x : 12 * x + 12, :] = moved[16 * th : 16 * th + 12, 0:WIN]
        for part in range(3):
            w3[part] = wqkv[:, part * C : (part + 1) * C]
        wt[...] = wqkv[...].astype(F32).T.astype(BF16)
        to_window = onehot(3, TOKENS, PIECES)
        pwt[...] = onehot(1, PIECES, TOKENS)
        pnt[...] = onehot(0, TOKENS, PIECES)

        for copy in halo:
            copy.wait_recv()
        arrived = dot(to_window, rbuf[...])
        xt[...] = arrived[:, 0:C]
        xg[...] = arrived[:, C : 2 * C].astype(BF16)

        head_of = lax.broadcasted_iota(jnp.int32, (1, C), 1) // DH
        eye = jnp.where(
            lax.broadcasted_iota(jnp.int32, (C, C), 0) == lax.broadcasted_iota(jnp.int32, (C, C), 1),
            1.0, 0.0,
        ).astype(BF16)

        def window(w, carry):
            r0 = pl.multiple_of(w * WIN, 16)
            t = lax.div(w, MEMBERS)
            x = xt[pl.ds(r0, WIN), :]
            g = xg[pl.ds(r0, WIN), :]
            centred = x - jnp.mean(x, axis=1, keepdims=True)
            inv_std = lax.rsqrt(jnp.mean(centred * centred, axis=1, keepdims=True) + EPS)
            x_hat = centred * inv_std
            normed = (x_hat * gain[...] + shift[...]).astype(BF16)
            q = dot(normed, w3[0]).astype(BF16)
            k = dot(normed, w3[1]).astype(BF16)
            v = dot(normed, w3[2]).astype(BF16)
            d_att = dot_nt(g, wproj[...]).astype(BF16)
            qkvt[0 : 3 * C, :] = dot_nt(wt[...], normed).astype(BF16)
            qkvt[3 * C : 4 * C, :] = dot_nt(wproj[...], g).astype(BF16)
            for h in range(HEADS):
                th = t * HEADS + h
                mine = head_of == h
                zero = jnp.zeros_like(q)
                s = dot_nt(jnp.where(mine, q, zero), k) * score_scale + bm[th]
                e = jnp.exp(s - jnp.max(s, axis=1, keepdims=True))
                p = e * (1.0 / jnp.sum(e, axis=1, keepdims=True))
                pb = p.astype(BF16)
                d_p = dot_nt(jnp.where(mine, d_att, zero), v)
                lo = h * DH
                ot[lo : lo + DH, :] = dot_nt(qkvt[2 * C + lo : 2 * C + lo + DH, :], pb).astype(BF16)
                dqt[2 * C + lo : 2 * C + lo + DH, :] = dot(
                    qkvt[3 * C + lo : 3 * C + lo + DH, :], pb
                ).astype(BF16)
                ds = p * (d_p - jnp.sum(p * d_p, axis=1, keepdims=True))
                at = pl.multiple_of(th * 16, 16)
                for xx in range(WW):
                    dacc[xx, pl.ds(at, 12), :] += ds[12 * xx : 12 * xx + 12, :]
                sc = (ds * score_scale).astype(BF16)
                dqt[lo : lo + DH, :] = dot_nt(qkvt[C + lo : C + lo + DH, :], sc).astype(BF16)
                dqt[C + lo : C + lo + DH, :] = dot(qkvt[lo : lo + DH, :], sc).astype(BF16)
            accp[...] += dot(ot[...], g)
            accq[...] += dot_nt(dot_nt(eye, normed).astype(BF16), dqt[...])
            d_normed = dot_tn(dqt[...], wt[...])
            accs[0:1, :] += jnp.sum(d_normed * x_hat, axis=0, keepdims=True)
            accs[1:2, :] += jnp.sum(d_normed, axis=0, keepdims=True)
            d_hat = d_normed * gain[...]
            m1 = jnp.mean(d_hat, axis=1, keepdims=True)
            m2 = jnp.mean(d_hat * x_hat, axis=1, keepdims=True)
            dx[pl.ds(r0, WIN), :] = (inv_std * (d_hat - m1 - x_hat * m2)).astype(BF16)
            return carry

        lax.fori_loop(0, TYPES * MEMBERS, window, 0)

        payf[...] = jnp.zeros_like(payf)
        payf[0, 0:C, :] = accq[:, 0:384]
        payf[1, 0:C, :] = jnp.concatenate([accq[:, 384:576], accp[...]], axis=1)
        payf[0, C : C + 8, 0:C] = accs[...]
        payb[...] = payf[...].astype(BF16)
        pair = remote(payb.at[1 - core], pairb, s_p, r_p, pair_dev)
        pair.start()

        sb2[...] = dot(pwt[...], dx[...]).astype(BF16)
        back = []
        for q in range(1, 8):
            part = pl.ds(PIECE_AT[q], PIECE_LEN[q])
            copy = remote(sb2.at[part], rb2.at[part], s_o.at[q], r_o.at[q], halo_dev(q, 1))
            copy.start()
            back.append(copy)
        rb2[0:112, :] = sb2[0:112, :]

        pair.wait_recv()
        rsrc[...] = (payf[core] + pairb[...].astype(F32)).astype(BF16)

        def block(ref, p):
            return ref.at[pl.ds(pl.multiple_of(p * 16, 16), 16)]

        def plane_copy(k):
            p = lax.rem(me_p + k, plane_n)
            return p, remote(
                block(rsrc, p), plb.at[k], s_1.at[k], r_1.at[k], plane_dev(p)
            )

        for k in range(1, plane_n):
            p, copy = plane_copy(k)
            pl.when(p < BLOCKS)(copy.start)

        folded = jnp.zeros((192, 384), F32)
        for x in range(WW):
            padded = jnp.concatenate([dacc[x], jnp.zeros((192, 384 - WIN), F32)], axis=1)
            off = 12 * (WW - 1 - x)
            folded = folded + (pltpu.roll(padded, off, 1) if off else padded)
        by_b = dot(onehot(6, 192, 192), folded.astype(BF16)).astype(BF16)
        for zj in range(WZ):
            pa, pb2, pc, pd = [dot(by_b, onehot(row + zj, 384, 256)) for row in (7, 9, 11, 13)]
            for zi in range(WZ):
                for u in range(2):
                    d = ((zi * WZ + zj) * 2 + u) * 2
                    b0 = (zi * WH + 3 * u) * 16
                    bmsg[d] = (pa[b0 : b0 + 16] + pb2[b0 + 16 : b0 + 32]).astype(BF16)
                    bmsg[d + 1] = (pc[b0 + 16 : b0 + 32] + pd[b0 + 32 : b0 + 48]).astype(BF16)
        bias = []
        for k in range(1, lon_n):
            dev = lon_dev(k)
            copy = remote(bmsg.at[dev["lon"]], brcv.at[k], s_b.at[k], r_b.at[k], dev)
            copy.start()
            bias.append(copy)

        def z_copy(k):
            return remote(zbuf.at[zz], zbuf.at[zz], s_2.at[k], r_2.at[k], z_dev(k))

        def z_from(k):
            z = lax.rem(zz + z_n - k, z_n)
            return remote(zbuf.at[z], zbuf.at[z], s_2.at[k], r_2.at[k], z_dev(k))

        @pl.when(me_p < BLOCKS)
        def _():
            part = rsrc[pl.ds(pl.multiple_of(me_p * 16, 16), 16), :].astype(F32)
            for k in range(1, plane_n):
                remote(block(rsrc, me_p), plb.at[k], s_1.at[k], r_1.at[k], pair_dev).wait_recv()
                part = part + plb[k].astype(F32)
            zbuf[zz] = part.astype(BF16)
            for k in range(1, z_n):
                z_copy(k).start()

        for copy in back:
            copy.wait_recv()
        ztok[...] = dot(pnt[...], rb2[...])
        for k in range(TOKENS // 24):
            for half in range(2):
                slab = 2 * k + half
                at = 24 * k + 12 * half
                out_tok[slab] = (cot[slab].astype(F32) + ztok[at : at + 12, :]).astype(BF16)

        def gather_copy(k):
            p = lax.rem(me_p + k, plane_n)
            mine = block(fbuf.at[core], me_p)
            return remote(mine, mine, s_3.at[k], r_3.at[k], plane_dev(p))

        def pair_copy(k, p, side):
            there = block(fbuf.at[side], p)
            return remote(there, there, s_4.at[k], r_4.at[k], pair_dev)

        @pl.when(me_p < BLOCKS)
        def _():
            for k in range(1, z_n):
                z_from(k).wait_recv()
            part = zbuf[0].astype(F32)
            for k in range(1, z_n):
                part = part + zbuf[k].astype(F32)
            fbuf[core, pl.ds(pl.multiple_of(me_p * 16, 16), 16), :] = (part * grad_scale).astype(BF16)
            for k in range(1, plane_n):
                gather_copy(k).start()
            pair_copy(0, me_p, core).start()

        sums = bmsg[o].astype(F32)
        for k in range(1, lon_n):
            bias[k - 1].wait_recv()
            sums = sums + brcv[k].astype(F32)
        for t in range(TYPES):
            out_bias[t] = sums[8 * t : 8 * t + 6, 0 : FOLD * 3 // 2]

        for k in range(1, plane_n):
            p = lax.rem(me_p + plane_n - k, plane_n)

            @pl.when(p < BLOCKS)
            def _():
                here = block(fbuf.at[core], p)
                remote(here, here, s_3.at[k], r_3.at[k], pair_dev).wait_recv()
                pair_copy(k, p, core).start()

        for k in range(plane_n):
            p = lax.rem(me_p + plane_n - k, plane_n)

            @pl.when(p < BLOCKS)
            def _():
                pair_copy(k, p, 1 - core).wait_recv()

        out_qkv[:, 0:384] = fbuf[0, 0:C, :].astype(F32)
        right = fbuf[1, 0:C, :].astype(F32)
        out_qkv[:, 384:576] = right[:, 0:C]
        out_proj[...] = right[:, C : 2 * C]
        norms = fbuf[0, C : C + 16, :].astype(F32)
        out_gain[...] = norms[0:1, 0:C]
        out_shift[...] = norms[1:2, 0:C]

        for copy in halo + back + bias:
            copy.wait_send()
        pair.wait_send()
        for k in range(1, plane_n):
            p, copy = plane_copy(k)
            pl.when(p < BLOCKS)(copy.wait_send)

        @pl.when(me_p < BLOCKS)
        def _():
            for k in range(1, z_n):
                z_copy(k).wait_send()
            for k in range(1, plane_n):
                gather_copy(k).wait_send()

        for k in range(plane_n):
            p = lax.rem(me_p + plane_n - k, plane_n)

            @pl.when(p < BLOCKS)
            def _():
                pair_copy(k, p, core).wait_send()

    sems = pltpu.SemaphoreType.DMA
    scratch = [
        pltpu.VMEM((TOKENS, C), F32),
        pltpu.VMEM((TOKENS, C), F32),
        pltpu.VMEM((PIECES, 2 * C), BF16),
        pltpu.VMEM((PIECES, 2 * C), BF16),
        pltpu.VMEM((TOKENS, C), F32),
        pltpu.VMEM((TOKENS, C), BF16),
        pltpu.VMEM((TOKENS, C), BF16),
        pltpu.VMEM((PIECES, C), BF16),
        pltpu.VMEM((PIECES, C), BF16),
        pltpu.VMEM((192, 512), F32),
        pltpu.VMEM((TYPES * HEADS, WIN, WIN), F32),
        pltpu.VMEM((WW, 192, WIN), F32),
        pltpu.VMEM((3, C, C), BF16),
        pltpu.VMEM((3 * C, C), BF16),
        pltpu.VMEM((16, 128), BF16),
        pltpu.VMEM((PIECES, TOKENS), BF16),
        pltpu.VMEM((TOKENS, PIECES), BF16),
        pltpu.VMEM((4 * C, WIN), BF16),
        pltpu.VMEM((3 * C, WIN), BF16),
        pltpu.VMEM((C, WIN), BF16),
        pltpu.VMEM((C, 3 * C), F32),
        pltpu.VMEM((C, C), F32),
        pltpu.VMEM((8, C), F32),
        pltpu.VMEM((2, 16 * BLOCKS, 384), F32),
        pltpu.VMEM((2, 16 * BLOCKS, 384), BF16),
        pltpu.VMEM((16 * BLOCKS, 384), BF16),
        pltpu.VMEM((16 * BLOCKS, 384), BF16),
        pltpu.VMEM((plane_n, 16, 384), BF16),
        pltpu.VMEM((z_n, 16, 384), BF16),
        pltpu.VMEM((2, 16 * BLOCKS, 384), BF16),
        pltpu.VMEM((16, 16, 256), BF16),
        pltpu.VMEM((16, 16, 256), BF16),
        sems((8,)), sems((8,)), sems((8,)), sems((8,)), sems, sems,
        sems((plane_n,)), sems((plane_n,)), sems((z_n,)), sems((z_n,)),
        sems((plane_n,)), sems((plane_n,)), sems((plane_n,)), sems((plane_n,)),
        sems((lon_n,)), sems((lon_n,)),
    ]
    return body, scratch


def solution(mesh):
    lon_n, lev_n, lat_n = (mesh.shape[name] for name in ("lon", "lev", "lat"))
    body, scratch = make_body(lon_n, lev_n, lat_n)
    index = index_rows()

    def local(tokens, cotangent, w_qkv, w_proj, ln_gain, ln_shift, bias_table, region_ids, lat_keep):
        slabs = (MEMBERS * LEVELS * ROWS, LONGS, C)
        vmem = pl.BlockSpec(memory_space=pltpu.VMEM)
        smem = pl.BlockSpec(memory_space=pltpu.SMEM)
        back, g_qkv, g_proj, g_gain, g_shift, g_bias = pl.pallas_call(
            body,
            out_shape=(
                jax.ShapeDtypeStruct(slabs, BF16),
                jax.ShapeDtypeStruct((C, 3 * C), F32),
                jax.ShapeDtypeStruct((C, C), F32),
                jax.ShapeDtypeStruct((1, C), F32),
                jax.ShapeDtypeStruct((1, C), F32),
                jax.ShapeDtypeStruct((TYPES, HEADS, FOLD * 3 // 2), F32),
            ),
            in_specs=[vmem] * 7 + [smem, smem, vmem],
            out_specs=(vmem,) * 6,
            scratch_shapes=scratch,
            compiler_params=pltpu.CompilerParams(
                collective_id=0, has_side_effects=True, vmem_limit_bytes=56 * 1024 * 1024
            ),
        )(
            tokens.reshape(slabs), cotangent.reshape(slabs), w_qkv, w_proj,
            ln_gain.reshape(1, C), ln_shift.reshape(1, C), bias_table,
            region_ids, lat_keep.reshape(1, ROWS), jnp.asarray(index),
        )
        return (
            back.reshape(tokens.shape), g_qkv, g_proj, g_gain.reshape(C), g_shift.reshape(C), g_bias,
        )

    return jax.shard_map(
        local,
        mesh=mesh,
        in_specs=(
            P(None, "lev", "lat", "lon", None),
            P(None, "lev", "lat", "lon", None),
            P(), P(), P(), P(),
            P(("lev", "lat"), None, None),
            P("lev", "lat"),
            P("lat"),
        ),
        out_specs=(
            P(None, "lev", "lat", "lon", None),
            P(), P(), P(), P(),
            P(("lev", "lat"), None, "lon"),
        ),
        check_vma=False,
    )
```

```python
import math

import jax
import jax.numpy as jnp
import numpy as np
from jax import lax
from jax.experimental import pallas as pl
from jax.experimental.pallas import tpu as pltpu
from jax.sharding import PartitionSpec as P

MESH = pl.DeviceIdType.MESH
F32 = jnp.float32
BF16 = jnp.bfloat16

HEADS = 6
WZ = 2
WH = 6
WW = 12
MEMBERS = 2
LEVELS = 2
ROWS = 12
LONGS = 12
C = 192
DH = C // HEADS
WIN = WZ * WH * WW
TYPES = 2
TOKENS = MEMBERS * LEVELS * ROWS * LONGS
SPAN = 2 * WW - 1
FOLD = WH * SPAN
PIECES = 640
MASKED = -1000000000.0
EPS = 1e-05

PIECE_AT = [0, 112, 224, 336, 448, 496, 544, 592]
PIECE_LEN = [112, 112, 112, 112, 48, 48, 48, 48]
BLOCKS = 13


def piece_steps(q):
    return (q // 2) % 2, q // 4, q % 2


def index_rows():
    out = np.full((16, PIECES), -1, np.int32)
    of_natural = np.full(PIECES, -1, np.int32)
    of_window = np.full(PIECES, -1, np.int32)
    for q in range(8):
        dz, dh, dw = piece_steps(q)
        rows = 3 if dh else 9
        for m in range(MEMBERS):
            for hh in range(rows):
                for ww in range(6):
                    s = PIECE_AT[q] + (m * rows + hh) * 6 + ww
                    lev = 1 - dz
                    row = hh if dh else 3 + hh
                    lon = ww if dw else 6 + ww
                    of_natural[s] = ((m * ROWS + row) * LONGS + lon) * LEVELS + lev
                    there = 9 + hh if dh else hh
                    t, h = there // WH, there % WH
                    w = 6 + ww if dw else ww
                    of_window[s] = (t * MEMBERS + m) * WIN + w * 12 + dz * WH + h
    out[0] = of_natural
    out[3] = of_window
    for s in range(PIECES):
        if of_natural[s] >= 0:
            out[2, of_natural[s]] = s
            out[1, of_window[s]] = s
    for rr in range(SPAN):
        for zj in range(WZ):
            for hj in range(WH):
                out[4, (rr * WZ + zj) * WH + hj] = zj * 256 + hj * SPAN + SPAN - 1 - rr
    for b in range(12):
        for t in range(TYPES):
            for h in range(HEADS):
                th, slot = t * HEADS + h, h * TYPES + t
                out[5, b * 16 + slot] = th * 16 + b
                out[6, th * 16 + b] = b * 16 + slot
    for zj in range(WZ):
        for hj in range(WH):
            for r in range(SPAN):
                src = ((SPAN - 1 - r) * WZ + zj) * WH + hj
                flat = hj * SPAN + r
                out[7 + zj, flat] = src
                if hj < 3:
                    out[9 + zj, FOLD + flat] = src
                else:
                    out[11 + zj, flat - FOLD // 2] = src
                out[13 + zj, FOLD // 2 + flat] = src
    out[15, :384] = np.arange(384) % 12
    return out


def dot(a, b):
    return lax.dot_general(a, b, (((1,), (0,)), ((), ())), preferred_element_type=F32)


def dot_nt(a, b):
    return lax.dot_general(a, b, (((1,), (1,)), ((), ())), preferred_element_type=F32)


def dot_tn(a, b):
    return lax.dot_general(a, b, (((0,), (0,)), ((), ())), preferred_element_type=F32)


def make_body(lon_n, lev_n, lat_n):
    z_n = lon_n // 2
    y_n = lat_n // 2
    plane_n = 2 * y_n * lev_n
    total = MEMBERS * LEVELS * ROWS * LONGS * lon_n * lev_n * lat_n
    grad_scale = 1.0 / math.sqrt(total)
    score_scale = DH ** (-0.5)

    def body(
        tok, cot, wqkv, wproj, gain, shift, table, reg, keep, idx,
        out_tok, out_qkv, out_proj, out_gain, out_shift, out_bias,
        sbuf, rbuf, xt, xg, dx, sb2, rb2,
        xk, bm, dacc, by_x, w3, wt, pwt, pnt, qkvt, dqt, ot,
        accq, accp, accs, payf, payb, pairb, rsrc, plb, zbuf, fbuf, bmsg, brcv,
        s_h, r_h, s_o, r_o, s_p, r_p, s_1, r_1, s_2, r_2, s_3, r_3, s_4, r_4, s_b, r_b,
    ):
        o = lax.axis_index("lon")
        lv = lax.axis_index("lev")
        la = lax.axis_index("lat")
        core = lax.rem(la, 2)
        ylo = lax.div(la, 2)
        zz = lax.rem(o, z_n)
        yhi = lax.div(o, z_n)
        me_p = (yhi * y_n + ylo) * lev_n + lv

        def halo_dev(q, sign):
            dz, dh, dw = piece_steps(q)
            return {
                "lon": lax.rem(o + sign * dw + lon_n, lon_n),
                "lev": lax.rem(lv + sign * dz + lev_n, lev_n),
                "lat": lax.rem(la + sign * dh + lat_n, lat_n),
            }

        def plane_dev(p):
            ph = lax.div(p, y_n * lev_n)
            rest = lax.rem(p, y_n * lev_n)
            return {
                "lon": ph * z_n + zz,
                "lev": lax.rem(rest, lev_n),
                "lat": lax.div(rest, lev_n) * 2 + core,
            }

        def z_dev(k):
            return {"lon": yhi * z_n + lax.rem(zz + k, z_n), "lev": lv, "lat": la}

        def lon_dev(k):
            return {"lon": lax.rem(o + k, lon_n), "lev": lv, "lat": la}

        pair_dev = {"lon": o, "lev": lv, "lat": ylo * 2 + 1 - core}

        def remote(src, dst, ssem, rsem, dev):
            return pltpu.make_async_remote_copy(
                src_ref=src, dst_ref=dst, send_sem=ssem, recv_sem=rsem,
                device_id=dev, device_id_type=MESH,
            )

        partners = [halo_dev(q, s) for q in range(1, 8) for s in (-1, 1)]
        partners.append(pair_dev)
        partners += [plane_dev(lax.rem(me_p + k, plane_n)) for k in range(1, plane_n)]
        partners += [lon_dev(k) for k in range(1, lon_n)]
        barrier = pltpu.get_barrier_semaphore()
        for dev in partners:
            pl.semaphore_signal(barrier, inc=1, device_id=dev, device_id_type=MESH)

        def onehot(row, height, width):
            pick = lax.broadcasted_iota(jnp.int32, (height, width), 0) == idx[row : row + 1, 0:width]
            return jnp.where(pick, 1.0, 0.0).astype(BF16)

        own = cot[...].reshape(TOKENS, C).astype(F32)
        line = LONGS * LEVELS
        kept = jnp.concatenate(
            [
                own[k * line : (k + 1) * line] * keep[0, k % ROWS].astype(F32)
                for k in range(MEMBERS * ROWS)
            ],
            axis=0,
        )
        gather = onehot(2, PIECES, TOKENS)
        piece_tok = dot(gather, tok[...].reshape(TOKENS, C))
        piece_cot = dot(gather, kept.astype(BF16))
        sbuf[...] = jnp.concatenate([piece_tok, piece_cot], axis=1).astype(BF16)

        pl.semaphore_wait(barrier, len(partners))
        halo = []
        for q in range(1, 8):
            part = pl.ds(PIECE_AT[q], PIECE_LEN[q])
            copy = remote(sbuf.at[part], rbuf.at[part], s_h.at[q], r_h.at[q], halo_dev(q, -1))
            copy.start()
            halo.append(copy)
        rbuf[0:112, :] = sbuf[0:112, :]

        accq[...] = jnp.zeros_like(accq)
        accp[...] = jnp.zeros_like(accp)
        accs[...] = jnp.zeros_like(accs)
        xk[...] = jnp.zeros_like(xk)
        for zi in range(WZ):
            for zj in range(WZ):
                for hi in range(WH):
                    kappa = (zi * WZ + zj) * WH + hi
                    b = zi * WH + hi
                    xk[b * 16 : b * 16 + 12, zj * 256 : zj * 256 + FOLD] = table[
                        :, :, kappa * FOLD : (kappa + 1) * FOLD
                    ].reshape(TYPES * HEADS, FOLD)
        to_th = onehot(5, 192, 192)
        to_lane = onehot(4, 512, 384)
        rest = xk[...]
        wide = jnp.zeros((192, 384), F32)
        for _ in range(3):
            term = rest.astype(BF16)
            rest = rest - term.astype(F32)
            wide = wide + dot(dot(to_th, term).astype(BF16), to_lane)
        lane_a = idx[15:16, 0:384]
        row_b = lax.broadcasted_iota(jnp.int32, (16, 384), 0)
        masked = []
        for t in range(TYPES):
            reg_a = jnp.zeros((16, 384), jnp.int32)
            reg_b = jnp.zeros((16, 384), jnp.int32)
            for z in range(WZ):
                for h in range(WH):
                    ident = reg[z, t * WH + h]
                    reg_a = jnp.where(lane_a == z * WH + h, ident, reg_a)
                    reg_b = jnp.where(row_b == z * WH + h, ident, reg_b)
            for h in range(HEADS):
                th = t * HEADS + h
                masked.append(jnp.where(reg_a == reg_b, wide[th * 16 : th * 16 + 16], MASKED))
        wide = jnp.concatenate(masked, axis=0)
        for x in range(WW):
            moved = pltpu.roll(wide, (384 - 12 * (WW - 1 - x)) % 384, 1) if x < WW - 1 else wide
            for th in range(TYPES * HEADS):
                dacc[th, 12 * x : 12 * x + 12, :] = moved[16 * th : 16 * th + 12, 0:WIN]
        for th in range(TYPES * HEADS):
            bm[th] = dacc[th].T
        dacc[...] = jnp.zeros_like(dacc)
        dx[...] = jnp.zeros_like(dx)
        for part in range(3):
            w3[part] = wqkv[:, part * C : (part + 1) * C]
        wt[...] = wqkv[...].astype(F32).T.astype(BF16)
        to_window = onehot(3, TOKENS, PIECES)
        pwt[...] = onehot(1, PIECES, TOKENS)
        pnt[...] = onehot(0, TOKENS, PIECES)

        for copy in halo:
            copy.wait_recv()
        arrived = dot(to_window, rbuf[...])
        xt[...] = arrived[:, 0:C]
        xg[...] = arrived[:, C : 2 * C].astype(BF16)

        head_of = lax.broadcasted_iota(jnp.int32, (1, C), 1) // DH
        eye = jnp.where(
            lax.broadcasted_iota(jnp.int32, (C, C), 0) == lax.broadcasted_iota(jnp.int32, (C, C), 1),
            1.0, 0.0,
        ).astype(BF16)

        ones = jnp.ones((C, C), BF16)

        def mean(rows):
            return dot(rows.astype(BF16), ones) * (1.0 / C)

        def window(w, carry):
            r0 = pl.multiple_of(w * WIN, 16)
            t = lax.div(w, MEMBERS)
            x = xt[pl.ds(r0, WIN), :]
            g = xg[pl.ds(r0, WIN), :]
            centred = x - mean(x)
            inv_std = lax.rsqrt(mean(centred * centred) + EPS)
            x_hat = centred * inv_std
            normed = (x_hat * gain[...] + shift[...]).astype(BF16)
            q = dot(normed, w3[0]).astype(BF16)
            k = dot(normed, w3[1]).astype(BF16)
            v = dot(normed, w3[2]).astype(BF16)
            d_att = dot_nt(g, wproj[...]).astype(BF16)
            qkvt[0 : 3 * C, :] = dot_nt(wt[...], normed).astype(BF16)
            qkvt[3 * C : 4 * C, :] = dot_nt(wproj[...], g).astype(BF16)
            zero = jnp.zeros_like(k)
            for h in range(HEADS):
                th = t * HEADS + h
                mine = head_of == h
                s = dot_nt(jnp.where(mine, k, zero), q) * score_scale + bm[th]
                e = jnp.exp(s - jnp.max(s, axis=0, keepdims=True))
                p = e * (1.0 / jnp.sum(e, axis=0, keepdims=True))
                pb = p.astype(BF16)
                d_p = dot_nt(jnp.where(mine, v, zero), d_att)
                lo = h * DH
                q_h, k_h, v_h, a_h = (qkvt[part * C + lo : part * C + lo + DH, :] for part in range(4))
                ot[lo : lo + DH, :] = dot(v_h, pb).astype(BF16)
                dqt[2 * C + lo : 2 * C + lo + DH, :] = dot_nt(a_h, pb).astype(BF16)
                ds = p * (d_p - jnp.sum(p * d_p, axis=0, keepdims=True))
                dacc[th] += ds
                sc = (ds * score_scale).astype(BF16)
                dqt[lo : lo + DH, :] = dot(k_h, sc).astype(BF16)
                dqt[C + lo : C + lo + DH, :] = dot_nt(q_h, sc).astype(BF16)
            accp[...] += dot(ot[...], g)
            accq[...] += dot_nt(dot_nt(eye, normed).astype(BF16), dqt[...])
            d_normed = dot_tn(dqt[...], wt[...])
            accs[0:1, :] += jnp.sum(d_normed * x_hat, axis=0, keepdims=True)
            accs[1:2, :] += jnp.sum(d_normed, axis=0, keepdims=True)
            d_hat = d_normed * gain[...]
            d_x = inv_std * (d_hat - mean(d_hat) - x_hat * mean(d_hat * x_hat))
            dx[pl.ds(r0, WIN), 0:C] = d_x.astype(BF16)
            return carry

        lax.fori_loop(0, TYPES * MEMBERS, window, 0)

        payf[...] = jnp.zeros_like(payf)
        payf[0, 0:C, :] = accq[:, 0:384]
        payf[1, 0:C, :] = jnp.concatenate([accq[:, 384:576], accp[...]], axis=1)
        payf[0, C : C + 8, 0:C] = accs[...]
        payb[...] = payf[...].astype(BF16)
        pair = remote(payb.at[1 - core], pairb, s_p, r_p, pair_dev)
        pair.start()

        sb2[...] = dot(pwt[...], dx[...]).astype(BF16)
        back = []
        for q in range(1, 8):
            part = pl.ds(PIECE_AT[q], PIECE_LEN[q])
            copy = remote(sb2.at[part], rb2.at[part], s_o.at[q], r_o.at[q], halo_dev(q, 1))
            copy.start()
            back.append(copy)
        rb2[0:112, :] = sb2[0:112, :]

        pair.wait_recv()
        rsrc[...] = (payf[core] + pairb[...].astype(F32)).astype(BF16)

        def block(ref, p):
            return ref.at[pl.ds(pl.multiple_of(p * 16, 16), 16)]

        def plane_copy(k):
            p = lax.rem(me_p + k, plane_n)
            return p, remote(
                block(rsrc, p), plb.at[k], s_1.at[k], r_1.at[k], plane_dev(p)
            )

        for k in range(1, plane_n):
            p, copy = plane_copy(k)
            pl.when(p < BLOCKS)(copy.start)

        by_x[...] = jnp.zeros_like(by_x)
        folded = jnp.zeros((192, 384), F32)
        for th in range(TYPES * HEADS):
            turned = dacc[th].T
            for x in range(WW):
                by_x[x, 16 * th : 16 * th + 12, :] = turned[12 * x : 12 * x + 12, :]
        for x in range(WW):
            padded = jnp.concatenate([by_x[x], jnp.zeros((192, 384 - WIN), F32)], axis=1)
            off = 12 * (WW - 1 - x)
            folded = folded + (pltpu.roll(padded, off, 1) if off else padded)
        by_b = dot(onehot(6, 192, 192), folded.astype(BF16)).astype(BF16)
        for zj in range(WZ):
            pa, pb2, pc, pd = [dot(by_b, onehot(row + zj, 384, 256)) for row in (7, 9, 11, 13)]
            for zi in range(WZ):
                for u in range(2):
                    d = ((zi * WZ + zj) * 2 + u) * 2
                    b0 = (zi * WH + 3 * u) * 16
                    bmsg[d] = (pa[b0 : b0 + 16] + pb2[b0 + 16 : b0 + 32]).astype(BF16)
                    bmsg[d + 1] = (pc[b0 + 16 : b0 + 32] + pd[b0 + 32 : b0 + 48]).astype(BF16)
        bias = []
        for k in range(1, lon_n):
            dev = lon_dev(k)
            copy = remote(bmsg.at[dev["lon"]], brcv.at[k], s_b.at[k], r_b.at[k], dev)
            copy.start()
            bias.append(copy)

        def z_copy(k):
            return remote(zbuf.at[zz], zbuf.at[zz], s_2.at[k], r_2.at[k], z_dev(k))

        def z_from(k):
            z = lax.rem(zz + z_n - k, z_n)
            return remote(zbuf.at[z], zbuf.at[z], s_2.at[k], r_2.at[k], z_dev(k))

        @pl.when(me_p < BLOCKS)
        def _():
            part = rsrc[pl.ds(pl.multiple_of(me_p * 16, 16), 16), :].astype(F32)
            for k in range(1, plane_n):
                remote(block(rsrc, me_p), plb.at[k], s_1.at[k], r_1.at[k], pair_dev).wait_recv()
                part = part + plb[k].astype(F32)
            zbuf[zz] = part.astype(BF16)
            for k in range(1, z_n):
                z_copy(k).start()

        for copy in back:
            copy.wait_recv()
        returned = dot(pnt[...], rb2[...])[:, 0:C]
        out_tok[...] = (own + returned).reshape(TOKENS // 2, 2, C).astype(BF16)

        def gather_copy(k):
            p = lax.rem(me_p + k, plane_n)
            mine = block(fbuf.at[core], me_p)
            return remote(mine, mine, s_3.at[k], r_3.at[k], plane_dev(p))

        def pair_copy(k, p, side):
            there = block(fbuf.at[side], p)
            return remote(there, there, s_4.at[k], r_4.at[k], pair_dev)

        @pl.when(me_p < BLOCKS)
        def _():
            for k in range(1, z_n):
                z_from(k).wait_recv()
            part = zbuf[0].astype(F32)
            for k in range(1, z_n):
                part = part + zbuf[k].astype(F32)
            fbuf[core, pl.ds(pl.multiple_of(me_p * 16, 16), 16), :] = (part * grad_scale).astype(BF16)
            for k in range(1, plane_n):
                gather_copy(k).start()
            pair_copy(0, me_p, core).start()

        sums = bmsg[o].astype(F32)
        for k in range(1, lon_n):
            bias[k - 1].wait_recv()
            sums = sums + brcv[k].astype(F32)
        out_bias[...] = sums[0 : TYPES * HEADS, 0 : FOLD * 3 // 2].reshape(HEADS, TYPES, FOLD * 3 // 2)

        for k in range(1, plane_n):
            p = lax.rem(me_p + plane_n - k, plane_n)

            @pl.when(p < BLOCKS)
            def _():
                here = block(fbuf.at[core], p)
                remote(here, here, s_3.at[k], r_3.at[k], pair_dev).wait_recv()
                pair_copy(k, p, core).start()

        for k in range(plane_n):
            p = lax.rem(me_p + plane_n - k, plane_n)

            @pl.when(p < BLOCKS)
            def _():
                pair_copy(k, p, 1 - core).wait_recv()

        out_qkv[:, 0:384] = fbuf[0, 0:C, :].astype(F32)
        right = fbuf[1, 0:C, :].astype(F32)
        out_qkv[:, 384:576] = right[:, 0:C]
        out_proj[...] = right[:, C : 2 * C]
        norms = fbuf[0, C : C + 16, :].astype(F32)
        out_gain[...] = norms[0:1, 0:C]
        out_shift[...] = norms[1:2, 0:C]

        for copy in halo + back + bias:
            copy.wait_send()
        pair.wait_send()
        for k in range(1, plane_n):
            p, copy = plane_copy(k)
            pl.when(p < BLOCKS)(copy.wait_send)

        @pl.when(me_p < BLOCKS)
        def _():
            for k in range(1, z_n):
                z_copy(k).wait_send()
            for k in range(1, plane_n):
                gather_copy(k).wait_send()

        for k in range(plane_n):
            p = lax.rem(me_p + plane_n - k, plane_n)

            @pl.when(p < BLOCKS)
            def _():
                pair_copy(k, p, core).wait_send()

    sems = pltpu.SemaphoreType.DMA
    scratch = [
        pltpu.VMEM((PIECES, 2 * C), BF16),
        pltpu.VMEM((PIECES, 2 * C), BF16),
        pltpu.VMEM((TOKENS, C), F32),
        pltpu.VMEM((TOKENS, C), BF16),
        pltpu.VMEM((TOKENS, 256), BF16),
        pltpu.VMEM((PIECES, 256), BF16),
        pltpu.VMEM((PIECES, 256), BF16),
        pltpu.VMEM((192, 512), F32),
        pltpu.VMEM((TYPES * HEADS, WIN, WIN), F32),
        pltpu.VMEM((TYPES * HEADS, WIN, WIN), F32),
        pltpu.VMEM((WW, 192, WIN), F32),
        pltpu.VMEM((3, C, C), BF16),
        pltpu.VMEM((3 * C, C), BF16),
        pltpu.VMEM((PIECES, TOKENS), BF16),
        pltpu.VMEM((TOKENS, PIECES), BF16),
        pltpu.VMEM((4 * C, WIN), BF16),
        pltpu.VMEM((3 * C, WIN), BF16),
        pltpu.VMEM((C, WIN), BF16),
        pltpu.VMEM((C, 3 * C), F32),
        pltpu.VMEM((C, C), F32),
        pltpu.VMEM((8, C), F32),
        pltpu.VMEM((2, 16 * BLOCKS, 384), F32),
        pltpu.VMEM((2, 16 * BLOCKS, 384), BF16),
        pltpu.VMEM((16 * BLOCKS, 384), BF16),
        pltpu.VMEM((16 * BLOCKS, 384), BF16),
        pltpu.VMEM((plane_n, 16, 384), BF16),
        pltpu.VMEM((z_n, 16, 384), BF16),
        pltpu.VMEM((2, 16 * BLOCKS, 384), BF16),
        pltpu.VMEM((16, 16, 256), BF16),
        pltpu.VMEM((16, 16, 256), BF16),
        sems((8,)), sems((8,)), sems((8,)), sems((8,)), sems, sems,
        sems((plane_n,)), sems((plane_n,)), sems((z_n,)), sems((z_n,)),
        sems((plane_n,)), sems((plane_n,)), sems((plane_n,)), sems((plane_n,)),
        sems((lon_n,)), sems((lon_n,)),
    ]
    return body, scratch


def hand_over(*refs):
    for source, target in zip(refs[:6], refs[6:]):
        target[...] = source[...]


def solution(mesh):
    lon_n, lev_n, lat_n = (mesh.shape[name] for name in ("lon", "lev", "lat"))
    body, scratch = make_body(lon_n, lev_n, lat_n)
    index = index_rows()

    def local(tokens, cotangent, w_qkv, w_proj, ln_gain, ln_shift, bias_table, region_ids, lat_keep):
        pairs = (TOKENS // LEVELS, LEVELS, C)
        vmem = pl.BlockSpec(memory_space=pltpu.VMEM)
        smem = pl.BlockSpec(memory_space=pltpu.SMEM)
        shapes = (
            jax.ShapeDtypeStruct(pairs, BF16),
            jax.ShapeDtypeStruct((C, 3 * C), F32),
            jax.ShapeDtypeStruct((C, C), F32),
            jax.ShapeDtypeStruct((1, C), F32),
            jax.ShapeDtypeStruct((1, C), F32),
            jax.ShapeDtypeStruct((HEADS, TYPES, FOLD * 3 // 2), F32),
        )
        results = pl.pallas_call(
            body,
            out_shape=shapes,
            in_specs=[vmem] * 7 + [smem, smem, vmem],
            out_specs=(vmem,) * 6,
            scratch_shapes=scratch,
            compiler_params=pltpu.CompilerParams(
                collective_id=0, has_side_effects=True, vmem_limit_bytes=40 * 1024 * 1024
            ),
        )(
            tokens.transpose(0, 2, 3, 1, 4).reshape(pairs),
            cotangent.transpose(0, 2, 3, 1, 4).reshape(pairs),
            w_qkv, w_proj, ln_gain.reshape(1, C), ln_shift.reshape(1, C),
            bias_table.transpose(1, 0, 2), region_ids, lat_keep.reshape(1, ROWS), jnp.asarray(index),
        )
        back, g_qkv, g_proj, g_gain, g_shift, g_bias = pl.pallas_call(
            hand_over,
            out_shape=shapes,
            in_specs=[vmem] * 6,
            out_specs=(vmem,) * 6,
        )(*results)
        back = back.reshape(MEMBERS, ROWS, LONGS, LEVELS, C).transpose(0, 3, 1, 2, 4)
        return back, g_qkv, g_proj, g_gain.reshape(C), g_shift.reshape(C), g_bias.transpose(1, 0, 2)

    return jax.shard_map(
        local,
        mesh=mesh,
        in_specs=(
            P(None, "lev", "lat", "lon", None),
            P(None, "lev", "lat", "lon", None),
            P(), P(), P(), P(),
            P(("lev", "lat"), None, None),
            P("lev", "lat"),
            P("lat"),
        ),
        out_specs=(
            P(None, "lev", "lat", "lon", None),
            P(), P(), P(), P(),
            P(("lev", "lat"), None, "lon"),
        ),
        check_vma=False,
    )
```

```python
import math

import jax
import jax.numpy as jnp
import numpy as np
from jax import lax
from jax.experimental import pallas as pl
from jax.experimental.pallas import tpu as pltpu
from jax.sharding import PartitionSpec as P

MESH = pl.DeviceIdType.MESH
F32 = jnp.float32
BF16 = jnp.bfloat16

HEADS = 6
WZ = 2
WH = 6
WW = 12
MEMBERS = 2
LEVELS = 2
ROWS = 12
LONGS = 12
C = 192
DH = C // HEADS
WIN = WZ * WH * WW
TYPES = 2
TOKENS = MEMBERS * LEVELS * ROWS * LONGS
SPAN = 2 * WW - 1
FOLD = WH * SPAN
PIECES = 704
MASKED = -1000000000.0
EPS = 1e-05

BAND_ROWS = (WH, 3, 3)
BAND_FROM = (3, 9, 0)
BAND_TO = (0, 6, 9)
PIECE = []
for band, padded in ((0, 80), (1, 48), (2, 48)):
    for steps in range(4):
        start = PIECE[-1][3] + PIECE[-1][4] if PIECE else 0
        PIECE.append((band, steps // 2, steps % 2, start, padded))
REMOTE = [q for q, piece in enumerate(PIECE) if piece[0] == 2 or piece[1] + piece[2] > 0]
OWN = [q for q in range(len(PIECE)) if q not in REMOTE]
TYPE_AT = (0, 320)
TYPE_ROWS = (320, 384)
HALF = TOKENS // TYPES
BLOCKS = 12
INPUTS = 10


def index_rows():
    out = np.full((24, PIECES), -1, np.int32)
    for band, dz, dw, start, _ in PIECE:
        rows = BAND_ROWS[band]
        for m in range(MEMBERS):
            for hh in range(rows):
                for ww in range(6):
                    s = start + (m * rows + hh) * 6 + ww
                    row = BAND_FROM[band] + hh
                    lon = ww if dw else 6 + ww
                    natural = ((m * ROWS + row) * LONGS + lon) * LEVELS + 1 - dz
                    t, h = divmod(BAND_TO[band] + hh, WH)
                    w = 6 + ww if dw else ww
                    i = m * WIN + w * 12 + dz * WH + h
                    out[0, s] = natural
                    out[2, natural] = s
                    out[16 + t, s - TYPE_AT[t]] = i
                    out[18 + t, i] = s - TYPE_AT[t]
    for rr in range(SPAN):
        for zj in range(WZ):
            for hj in range(WH):
                out[4, (rr * WZ + zj) * WH + hj] = zj * 256 + hj * SPAN + SPAN - 1 - rr
    for b in range(12):
        for t in range(TYPES):
            for h in range(HEADS):
                th, slot = t * HEADS + h, h * TYPES + t
                out[5, b * 16 + slot] = th * 16 + b
                out[6, th * 16 + b] = b * 16 + slot
    for zj in range(WZ):
        for hj in range(WH):
            for r in range(SPAN):
                src = ((SPAN - 1 - r) * WZ + zj) * WH + hj
                flat = hj * SPAN + r
                out[7 + zj, flat] = src
                if hj < 3:
                    out[9 + zj, FOLD + flat] = src
                else:
                    out[11 + zj, flat - FOLD // 2] = src
                out[13 + zj, FOLD // 2 + flat] = src
    out[15, :384] = np.arange(384) % 12
    return out


def dot(a, b):
    return lax.dot_general(a, b, (((1,), (0,)), ((), ())), preferred_element_type=F32)


def dot_nt(a, b):
    return lax.dot_general(a, b, (((1,), (1,)), ((), ())), preferred_element_type=F32)


def dot_tn(a, b):
    return lax.dot_general(a, b, (((0,), (0,)), ((), ())), preferred_element_type=F32)


def make_body(lon_n, lev_n, lat_n):
    z_n = lon_n // 2
    y_n = lat_n // 2
    plane_n = 2 * y_n * lev_n
    PLANE = sorted(
        [(dh, dy, dx) for dh in range(2) for dy in range(y_n) for dx in range(lev_n)],
        key=lambda step: -((2, 1)[step[1]] * step[0] + (1 - step[0]) * step[1] + min(step[2], lev_n - step[2])),
    )
    Z_STEPS = sorted(range(1, z_n), key=lambda k: -min(k, z_n - k))
    LON_STEPS = sorted(range(1, lon_n), key=lambda k: -min(k % z_n, z_n - k % z_n))
    PEERS = range(plane_n - 1)
    total = MEMBERS * LEVELS * ROWS * LONGS * lon_n * lev_n * lat_n
    grad_scale = 1.0 / math.sqrt(total)
    score_scale = DH ** (-0.5)

    def body(*refs):
        inputs, held = refs[:INPUTS], refs[INPUTS + 6 : 2 * INPUTS + 6]
        run(inputs, *held, *refs[INPUTS : INPUTS + 6], *refs[2 * INPUTS + 6 :])

    def run(
        inputs, tok, cot, wqkv, wproj, gain, shift, table, reg, keep, idx,
        out_tok, out_qkv, out_proj, out_gain, out_shift, out_bias,
        pick, sbuf, rbuf, xt, xg, dx, sb2, rb2,
        xk, bm, dacc, by_x, w3, wt, to_win, to_piece, pnt,
        payb, pairb, rsrc, plb, zbuf, fbuf, bmsg, brcv,
        s_h, r_h, s_o, r_o, s_p, r_p, s_1, r_1, s_2, r_2, s_3, r_3, s_4, r_4, s_b, r_b, s_i,
        gsv, gpl, gz, s_gp, r_gp, s_g1, r_g1, s_g2, r_g2,
    ):
        o = lax.axis_index("lon")
        lv = lax.axis_index("lev")
        la = lax.axis_index("lat")
        core = lax.rem(la, 2)
        ylo = lax.div(la, 2)
        zz = lax.rem(o, z_n)
        yhi = lax.div(o, z_n)
        me_p = (yhi * y_n + ylo) * lev_n + lv

        def halo_dev(dz, dh, dw, sign):
            return {
                "lon": lax.rem(o + sign * dw + lon_n, lon_n),
                "lev": lax.rem(lv + sign * dz + lev_n, lev_n),
                "lat": lax.rem(la + sign * dh + lat_n, lat_n),
            }

        def plane_dev(p):
            ph = lax.div(p, y_n * lev_n)
            rest = lax.rem(p, y_n * lev_n)
            return {
                "lon": ph * z_n + zz,
                "lev": lax.rem(rest, lev_n),
                "lat": lax.div(rest, lev_n) * 2 + core,
            }

        def plane_peer(k, sign):
            dh, dy, dx = PLANE[k]
            there = lax.rem(yhi + dh, 2) * y_n + lax.rem(ylo + dy, y_n)
            return there * lev_n + lax.rem(lv + sign * dx + lev_n, lev_n)

        def z_dev(k):
            return {"lon": yhi * z_n + lax.rem(zz + k, z_n), "lev": lv, "lat": la}

        def lon_dev(k):
            return {"lon": lax.rem(o + k, lon_n), "lev": lv, "lat": la}

        pair_dev = {"lon": o, "lev": lv, "lat": ylo * 2 + 1 - core}

        def remote(src, dst, ssem, rsem, dev):
            return pltpu.make_async_remote_copy(
                src_ref=src, dst_ref=dst, send_sem=ssem, recv_sem=rsem,
                device_id=dev, device_id_type=MESH,
            )

        def halo_copy(q, source, target, ssem, rsem, sign):
            band, dz, dw, start, rows = PIECE[q]
            part = pl.ds(start, rows)
            dev = halo_dev(dz, 1 if band == 2 else 0, dw, sign)
            return remote(source.at[part], target.at[part], ssem.at[q], rsem.at[q], dev)

        held = (tok, cot, wqkv, wproj, gain, shift, table, reg, keep, idx)
        loads = [
            pltpu.make_async_copy(source, target, s_i.at[k])
            for k, (source, target) in enumerate(zip(inputs, held))
        ]
        for k in (9, 0, 1, 8):
            loads[k].start()
        partners = [
            halo_dev(q // 4, q // 2 % 2, q % 2, sign) for q in range(1, 8) for sign in (-1, 1)
        ]
        partners += [lon_dev(k) for k in LON_STEPS]
        partners += [plane_dev(plane_peer(k, 1)) for k in PEERS]
        partners.append(pair_dev)
        barrier = pltpu.get_barrier_semaphore()
        for dev in partners:
            pl.semaphore_signal(barrier, inc=1, device_id=dev, device_id_type=MESH)
        for k in (6, 7, 2, 3, 4, 5):
            loads[k].start()

        def onehot(row, height, width):
            pick = lax.broadcasted_iota(jnp.int32, (height, width), 0) == idx[row : row + 1, 0:width]
            return jnp.where(pick, 1.0, 0.0).astype(BF16)

        loads[9].wait()
        pick[...] = onehot(2, PIECES, TOKENS)
        for k in (0, 1, 8):
            loads[k].wait()
        own = cot[...].reshape(TOKENS, C).astype(F32)
        line = LONGS * LEVELS
        kept = jnp.concatenate(
            [
                own[k * line : (k + 1) * line] * keep[0, k % ROWS].astype(F32)
                for k in range(MEMBERS * ROWS)
            ],
            axis=0,
        ).astype(BF16)
        piece_tok = dot(pick[...], tok[...].reshape(TOKENS, C))
        piece_cot = dot(pick[...], kept)
        sbuf[...] = jnp.concatenate([piece_tok, piece_cot], axis=1).astype(BF16)

        pl.semaphore_wait(barrier, len(partners))
        halo = {q: halo_copy(q, sbuf, rbuf, s_h, r_h, -1) for q in REMOTE}
        back = {q: halo_copy(q, sb2, rb2, s_o, r_o, 1) for q in REMOTE}
        for copy in halo.values():
            copy.start()
        for q in OWN:
            start, rows = PIECE[q][3:]
            rbuf[start : start + rows, :] = sbuf[start : start + rows, :]

        for k in (6, 7, 2, 3, 4, 5):
            loads[k].wait()
        xk[...] = jnp.zeros_like(xk)
        for zi in range(WZ):
            for zj in range(WZ):
                for hi in range(WH):
                    kappa = (zi * WZ + zj) * WH + hi
                    b = zi * WH + hi
                    xk[b * 16 : b * 16 + 12, zj * 256 : zj * 256 + FOLD] = table[
                        :, :, kappa * FOLD : (kappa + 1) * FOLD
                    ].reshape(TYPES * HEADS, FOLD)
        to_th = onehot(5, 192, 192)
        to_lane = onehot(4, 512, 384)
        rest = xk[...]
        wide = jnp.zeros((192, 384), F32)
        for _ in range(3):
            term = rest.astype(BF16)
            rest = rest - term.astype(F32)
            wide = wide + dot(dot(to_th, term).astype(BF16), to_lane)
        lane_a = idx[15:16, 0:384]
        row_b = lax.broadcasted_iota(jnp.int32, (16, 384), 0)
        masked = []
        for t in range(TYPES):
            reg_a = jnp.zeros((16, 384), jnp.int32)
            reg_b = jnp.zeros((16, 384), jnp.int32)
            for z in range(WZ):
                for h in range(WH):
                    ident = reg[z, t * WH + h]
                    reg_a = jnp.where(lane_a == z * WH + h, ident, reg_a)
                    reg_b = jnp.where(row_b == z * WH + h, ident, reg_b)
            for h in range(HEADS):
                th = t * HEADS + h
                masked.append(jnp.where(reg_a == reg_b, wide[th * 16 : th * 16 + 16], MASKED))
        wide = jnp.concatenate(masked, axis=0)
        for x in range(WW):
            moved = pltpu.roll(wide, (384 - 12 * (WW - 1 - x)) % 384, 1) if x < WW - 1 else wide
            for th in range(TYPES * HEADS):
                dacc[th, 12 * x : 12 * x + 12, :] = moved[16 * th : 16 * th + 12, 0:WIN]
        for th in range(TYPES * HEADS):
            bm[th] = dacc[th].T
        dacc[...] = jnp.zeros_like(dacc)
        dx[...] = jnp.zeros_like(dx)
        for part in range(3):
            w3[part] = wqkv[:, part * C : (part + 1) * C]
        wt[...] = wqkv[...].astype(F32).T.astype(BF16)
        for t in range(TYPES):
            part = slice(TYPE_AT[t], TYPE_AT[t] + TYPE_ROWS[t])
            to_win[:, part] = onehot(16 + t, HALF, TYPE_ROWS[t])
            to_piece[part, :] = onehot(18 + t, TYPE_ROWS[t], HALF)
        pnt[...] = onehot(0, TOKENS, PIECES)

        head_of = lax.broadcasted_iota(jnp.int32, (1, C), 1) // DH
        eye = jnp.where(
            lax.broadcasted_iota(jnp.int32, (C, C), 0) == lax.broadcasted_iota(jnp.int32, (C, C), 1),
            1.0, 0.0,
        ).astype(BF16)

        ones = jnp.ones((C, C), BF16)

        def mean(rows):
            return dot(rows.astype(BF16), ones) * (1.0 / C)

        def stack(rows):
            zero = jnp.zeros_like(rows)
            return jnp.concatenate([jnp.where(head_of == h, rows, zero) for h in range(HEADS)], axis=0)

        def unstack(rows):
            out = rows[0:WIN]
            for h in range(1, HEADS):
                out = jnp.where(head_of == h, rows[h * WIN : (h + 1) * WIN], out)
            return out.astype(BF16)

        def window(w):
            r0 = w * WIN
            t = w // MEMBERS
            x = xt[r0 : r0 + WIN, :]
            g = xg[r0 : r0 + WIN, :]
            centred = x - mean(x)
            inv_std = lax.rsqrt(mean(centred * centred) + EPS)
            x_hat = centred * inv_std
            normed = (x_hat * gain[...] + shift[...]).astype(BF16)
            normed_t = dot_nt(eye, normed).astype(BF16)
            q = dot(normed, w3[0]).astype(BF16)
            k = dot(normed, w3[1]).astype(BF16)
            v = dot(normed, w3[2]).astype(BF16)
            d_att = dot_nt(g, wproj[...]).astype(BF16)
            k_heads, v_heads = stack(k), stack(v)
            s_all = dot_nt(k_heads, q)
            dp_all = dot_nt(v_heads, d_att)
            probs, scaled = [], []
            for h in range(HEADS):
                th = t * HEADS + h
                s = s_all[h * WIN : (h + 1) * WIN] * score_scale + bm[th]
                e = jnp.exp(s - jnp.max(s, axis=0, keepdims=True))
                p = e * (1.0 / jnp.sum(e, axis=0, keepdims=True))
                d_p = dp_all[h * WIN : (h + 1) * WIN]
                ds = p * (d_p - jnp.sum(p * d_p, axis=0, keepdims=True))
                if w % MEMBERS == 0:
                    dacc[th] = ds
                else:
                    dacc[th] += ds
                probs.append(p.astype(BF16))
                scaled.append((ds * score_scale).astype(BF16))
            probs = jnp.concatenate(probs, axis=0)
            scaled = jnp.concatenate(scaled, axis=0)
            att_t = dot_tn(v_heads, probs).astype(BF16)
            dq_t = dot_tn(k_heads, scaled).astype(BF16)
            d_v = unstack(dot(probs, d_att))
            d_k = unstack(dot(scaled, q))
            sums = (dot_nt(normed_t, dq_t), dot(normed_t, d_k), dot(normed_t, d_v), dot(att_t, g))
            return sums, (x_hat, inv_std, dq_t, d_k, d_v)

        def norm_back(w, x_hat, inv_std, dq_t, d_k, d_v):
            d_normed = dot_tn(dq_t, wt[0:C, :]) + dot_nt(d_k, w3[1]) + dot_nt(d_v, w3[2])
            d_hat = d_normed * gain[...]
            d_x = inv_std * (d_hat - mean(d_hat) - x_hat * mean(d_hat * x_hat))
            dx[w * WIN : (w + 1) * WIN, 0:C] = d_x.astype(BF16)
            return (
                jnp.sum(d_normed * x_hat, axis=0, keepdims=True),
                jnp.sum(d_normed, axis=0, keepdims=True),
            )

        def arrive(t):
            for q in REMOTE:
                if (PIECE[q][0] > 0) == (t > 0):
                    halo[q].wait_recv()
            part = slice(TYPE_AT[t], TYPE_AT[t] + TYPE_ROWS[t])
            arrived = dot(to_win[:, part], rbuf[part, :])
            xt[t * HALF : (t + 1) * HALF, :] = arrived[:, 0:C]
            xg[t * HALF : (t + 1) * HALF, :] = arrived[:, C : 2 * C].astype(BF16)

        def pack(t):
            part = slice(TYPE_AT[t], TYPE_AT[t] + TYPE_ROWS[t])
            sb2[part, :] = dot(to_piece[part, :], dx[t * HALF : (t + 1) * HALF, :]).astype(BF16)

        def depart(t):
            for q in REMOTE:
                if (PIECE[q][0] > 0) == (t > 0):
                    back[q].start()

        arrive(0)
        done = [window(m) for m in range(MEMBERS)]
        arrive(1)
        done += [window(MEMBERS + m) for m in range(MEMBERS)]
        sum_q, sum_k, sum_v, sum_p = (
            sum((one[0][part] for one in done[1:]), done[0][0][part]) for part in range(4)
        )

        halves = (jnp.concatenate([sum_q, sum_k], axis=1), jnp.concatenate([sum_v, sum_p], axis=1))
        payb[0] = halves[0].astype(BF16)
        payb[1] = halves[1].astype(BF16)
        pair = remote(payb.at[1 - core], pairb, s_p, r_p, pair_dev)
        pair.start()

        norms = [norm_back(w, *one[1]) for w, one in enumerate(done)]
        gsv[core] = jnp.zeros((8, 128), F32)
        for row in range(2):
            both = sum((one[row] for one in norms[1:]), norms[0][row])
            gsv[core, 2 * row : 2 * row + 1, :] = both[:, 0:128]
            gsv[core, 2 * row + 1 : 2 * row + 2, 0 : C - 128] = both[:, 128:C]
        gs_pair = remote(gsv.at[core], gsv.at[core], s_gp, r_gp, pair_dev)
        gs_pair_from = remote(gsv.at[1 - core], gsv.at[1 - core], s_gp, r_gp, pair_dev)
        gs_pair.start()

        pair.wait_recv()
        kept_half = payb[core].astype(F32)
        rsrc[...] = (kept_half + pairb[...].astype(F32)).astype(BF16)

        def block(ref, p):
            return ref.at[pl.ds(pl.multiple_of(p * 16, 16), 16)]

        def plane_copy(k):
            p = plane_peer(k, 1)
            return p, remote(
                block(rsrc, p), plb.at[k], s_1.at[k], r_1.at[k], plane_dev(p)
            )

        for k in PEERS:
            p, copy = plane_copy(k)
            pl.when(p < BLOCKS)(copy.start)
        pack(0)
        pack(1)
        for q in OWN:
            start, rows = PIECE[q][3:]
            rb2[start : start + rows, :] = sb2[start : start + rows, :]

        gs_pair_from.wait_recv()
        gpl[me_p] = gsv[0] + gsv[1]

        def gs_plane(k, p):
            return remote(gpl.at[p], gpl.at[p], s_g1.at[k], r_g1.at[k], plane_dev(plane_peer(k, 1)))

        def gs_z(k, z):
            return remote(gz.at[z], gz.at[z], s_g2.at[k], r_g2.at[k], z_dev(k))

        for k in PEERS:
            gs_plane(k, me_p).start()

        depart(0)
        depart(1)

        by_x[...] = jnp.zeros_like(by_x)
        folded = jnp.zeros((192, 384), F32)
        for th in range(TYPES * HEADS):
            turned = dacc[th].T
            for x in range(WW):
                by_x[x, 16 * th : 16 * th + 12, :] = turned[12 * x : 12 * x + 12, :]
        for x in range(WW):
            padded = jnp.concatenate([by_x[x], jnp.zeros((192, 384 - WIN), F32)], axis=1)
            off = 12 * (WW - 1 - x)
            folded = folded + (pltpu.roll(padded, off, 1) if off else padded)
        by_b = dot(onehot(6, 192, 192), folded.astype(BF16)).astype(BF16)
        for zj in range(WZ):
            pa, pb2, pc, pd = [dot(by_b, onehot(row + zj, 384, 256)) for row in (7, 9, 11, 13)]
            for zi in range(WZ):
                for u in range(2):
                    d = ((zi * WZ + zj) * 2 + u) * 2
                    b0 = (zi * WH + 3 * u) * 16
                    bmsg[d] = (pa[b0 : b0 + 16] + pb2[b0 + 16 : b0 + 32]).astype(BF16)
                    bmsg[d + 1] = (pc[b0 + 16 : b0 + 32] + pd[b0 + 32 : b0 + 48]).astype(BF16)
        def z_copy(k):
            return remote(zbuf.at[zz], zbuf.at[zz], s_2.at[k], r_2.at[k], z_dev(k))

        def z_from(k):
            z = lax.rem(zz + z_n - k, z_n)
            return remote(zbuf.at[z], zbuf.at[z], s_2.at[k], r_2.at[k], z_dev(k))

        @pl.when(me_p < BLOCKS)
        def _():
            part = rsrc[pl.ds(pl.multiple_of(me_p * 16, 16), 16), :].astype(F32)
            for k in PEERS:
                remote(block(rsrc, me_p), plb.at[k], s_1.at[k], r_1.at[k], pair_dev).wait_recv()
                part = part + plb[k].astype(F32)
            zbuf[zz] = part.astype(BF16)
            for k in Z_STEPS:
                z_copy(k).start()

        def gather_copy(k):
            p = plane_peer(k, 1)
            mine = block(fbuf.at[core], me_p)
            return remote(mine, mine, s_3.at[k], r_3.at[k], plane_dev(p))

        def pair_copy(k, p, side):
            there = block(fbuf.at[side], p)
            return remote(there, there, s_4.at[k], r_4.at[k], pair_dev)

        @pl.when(me_p < BLOCKS)
        def _():
            for k in range(1, z_n):
                z_from(k).wait_recv()
            part = zbuf[0].astype(F32)
            for k in range(1, z_n):
                part = part + zbuf[k].astype(F32)
            fbuf[core, pl.ds(pl.multiple_of(me_p * 16, 16), 16), :] = (part * grad_scale).astype(BF16)
            for k in PEERS:
                gather_copy(k).start()
            pair_copy(plane_n - 1, me_p, core).start()

        for k in PEERS:
            gs_plane(k, plane_peer(k, -1)).wait_recv()
        part = gpl[0]
        for p in range(1, plane_n):
            part = part + gpl[p]
        gz[zz] = part
        for k in Z_STEPS:
            gs_z(k, zz).start()

        bias = []
        for k in LON_STEPS:
            dev = lon_dev(k)
            copy = remote(bmsg.at[dev["lon"]], brcv.at[k], s_b.at[k], r_b.at[k], dev)
            copy.start()
            bias.append(copy)


        for copy in back.values():
            copy.wait_recv()
        returned = dot(pnt[...], rb2[...])[:, 0:C]
        out_tok[...] = (own + returned).reshape(TOKENS // 2, 2, C).astype(BF16)

        for k in reversed(PEERS):
            p = plane_peer(k, -1)

            @pl.when(p < BLOCKS)
            def _():
                here = block(fbuf.at[core], p)
                remote(here, here, s_3.at[k], r_3.at[k], pair_dev).wait_recv()
                pair_copy(k, p, core).start()

        for k in Z_STEPS:
            gs_z(k, lax.rem(zz + z_n - k, z_n)).wait_recv()
        part = gz[0]
        for z in range(1, z_n):
            part = part + gz[z]
        part = part * grad_scale
        for row, out in enumerate((out_gain, out_shift)):
            out[:, 0:128] = part[2 * row : 2 * row + 1, :]
            out[:, 128:C] = part[2 * row + 1 : 2 * row + 2, 0 : C - 128]

        for k in range(plane_n):
            p = plane_peer(k, -1)

            @pl.when(p < BLOCKS)
            def _():
                pair_copy(k, p, 1 - core).wait_recv()

        out_qkv[:, 0:384] = fbuf[0, 0:C, :].astype(F32)
        right = fbuf[1, 0:C, :].astype(F32)
        out_qkv[:, 384:576] = right[:, 0:C]
        out_proj[...] = right[:, C : 2 * C]

        sums = bmsg[o].astype(F32)
        for copy in bias:
            copy.wait_recv()
        for k in range(1, lon_n):
            sums = sums + brcv[k].astype(F32)
        out_bias[...] = sums[0 : TYPES * HEADS, 0 : FOLD * 3 // 2].reshape(HEADS, TYPES, FOLD * 3 // 2)


        for copy in [*halo.values(), *back.values(), *bias]:
            copy.wait_send()
        pair.wait_send()
        gs_pair.wait_send()
        for k in PEERS:
            gs_plane(k, me_p).wait_send()
        for k in Z_STEPS:
            gs_z(k, zz).wait_send()
        for k in PEERS:
            p, copy = plane_copy(k)
            pl.when(p < BLOCKS)(copy.wait_send)

        @pl.when(me_p < BLOCKS)
        def _():
            for k in Z_STEPS:
                z_copy(k).wait_send()
            for k in PEERS:
                gather_copy(k).wait_send()

        for k in range(plane_n):
            p = plane_peer(k, -1)

            @pl.when(p < BLOCKS)
            def _():
                pair_copy(k, p, core).wait_send()

    sems = pltpu.SemaphoreType.DMA
    scratch = [
        pltpu.VMEM((TOKENS // 2, 2, C), BF16),
        pltpu.VMEM((TOKENS // 2, 2, C), BF16),
        pltpu.VMEM((C, 3 * C), BF16),
        pltpu.VMEM((C, C), BF16),
        pltpu.VMEM((1, C), F32),
        pltpu.VMEM((1, C), F32),
        pltpu.VMEM((HEADS, TYPES, WZ * WZ * WH * FOLD), F32),
        pltpu.SMEM((LEVELS, ROWS), jnp.int32),
        pltpu.SMEM((1, ROWS), jnp.int32),
        pltpu.VMEM((24, PIECES), jnp.int32),
        pltpu.VMEM((PIECES, TOKENS), BF16),
        pltpu.VMEM((PIECES, 2 * C), BF16),
        pltpu.VMEM((PIECES, 2 * C), BF16),
        pltpu.VMEM((TOKENS, C), F32),
        pltpu.VMEM((TOKENS, C), BF16),
        pltpu.VMEM((TOKENS, 256), BF16),
        pltpu.VMEM((PIECES, 256), BF16),
        pltpu.VMEM((PIECES, 256), BF16),
        pltpu.VMEM((192, 512), F32),
        pltpu.VMEM((TYPES * HEADS, WIN, WIN), F32),
        pltpu.VMEM((TYPES * HEADS, WIN, WIN), F32),
        pltpu.VMEM((WW, 192, WIN), F32),
        pltpu.VMEM((3, C, C), BF16),
        pltpu.VMEM((3 * C, C), BF16),
        pltpu.VMEM((HALF, PIECES), BF16),
        pltpu.VMEM((PIECES, HALF), BF16),
        pltpu.VMEM((TOKENS, PIECES), BF16),
        pltpu.VMEM((2, 16 * BLOCKS, 384), BF16),
        pltpu.VMEM((16 * BLOCKS, 384), BF16),
        pltpu.VMEM((16 * BLOCKS, 384), BF16),
        pltpu.VMEM((plane_n, 16, 384), BF16),
        pltpu.VMEM((z_n, 16, 384), BF16),
        pltpu.VMEM((2, 16 * BLOCKS, 384), BF16),
        pltpu.VMEM((16, 16, 256), BF16),
        pltpu.VMEM((16, 16, 256), BF16),
        *[sems((len(PIECE),))] * 4, sems, sems,
        sems((plane_n,)), sems((plane_n,)), sems((z_n,)), sems((z_n,)),
        sems((plane_n,)), sems((plane_n,)), sems((plane_n,)), sems((plane_n,)),
        sems((lon_n,)), sems((lon_n,)), sems((INPUTS,)),
        pltpu.VMEM((2, 8, 128), F32),
        pltpu.VMEM((plane_n, 8, 128), F32),
        pltpu.VMEM((z_n, 8, 128), F32),
        sems, sems, sems((plane_n,)), sems((plane_n,)), sems((z_n,)), sems((z_n,)),
    ]
    return body, scratch


def hand_over(*refs):
    for source, target in zip(refs[:6], refs[6:]):
        target[...] = source[...]


def solution(mesh):
    lon_n, lev_n, lat_n = (mesh.shape[name] for name in ("lon", "lev", "lat"))
    body, scratch = make_body(lon_n, lev_n, lat_n)
    index = index_rows()

    def local(tokens, cotangent, w_qkv, w_proj, ln_gain, ln_shift, bias_table, region_ids, lat_keep):
        pairs = (TOKENS // LEVELS, LEVELS, C)
        vmem = pl.BlockSpec(memory_space=pltpu.VMEM)
        shapes = (
            jax.ShapeDtypeStruct(pairs, BF16),
            jax.ShapeDtypeStruct((C, 3 * C), F32),
            jax.ShapeDtypeStruct((C, C), F32),
            jax.ShapeDtypeStruct((1, C), F32),
            jax.ShapeDtypeStruct((1, C), F32),
            jax.ShapeDtypeStruct((HEADS, TYPES, FOLD * 3 // 2), F32),
        )
        results = pl.pallas_call(
            body,
            out_shape=tuple(pltpu.VMEM(s.shape, s.dtype) for s in shapes),
            in_specs=[pl.BlockSpec(memory_space=pl.ANY)] * INPUTS,
            out_specs=(vmem,) * 6,
            scratch_shapes=scratch,
            compiler_params=pltpu.CompilerParams(
                collective_id=0, has_side_effects=True, vmem_limit_bytes=60 * 1024 * 1024
            ),
        )(
            tokens.transpose(0, 2, 3, 1, 4).reshape(pairs),
            cotangent.transpose(0, 2, 3, 1, 4).reshape(pairs),
            w_qkv, w_proj, ln_gain.reshape(1, C), ln_shift.reshape(1, C),
            bias_table.transpose(1, 0, 2), region_ids, lat_keep.reshape(1, ROWS), jnp.asarray(index),
        )
        back, g_qkv, g_proj, g_gain, g_shift, g_bias = pl.pallas_call(
            hand_over,
            out_shape=shapes,
            in_specs=[vmem] * 6,
            out_specs=(vmem,) * 6,
            compiler_params=pltpu.CompilerParams(vmem_limit_bytes=8 * 1024 * 1024),
        )(*results)
        back = back.reshape(MEMBERS, ROWS, LONGS, LEVELS, C).transpose(0, 3, 1, 2, 4)
        return back, g_qkv, g_proj, g_gain.reshape(C), g_shift.reshape(C), g_bias.transpose(1, 0, 2)

    return jax.shard_map(
        local,
        mesh=mesh,
        in_specs=(
            P(None, "lev", "lat", "lon", None),
            P(None, "lev", "lat", "lon", None),
            P(), P(), P(), P(),
            P(("lev", "lat"), None, None),
            P("lev", "lat"),
            P("lat"),
        ),
        out_specs=(
            P(None, "lev", "lat", "lon", None),
            P(), P(), P(), P(),
            P(("lev", "lat"), None, "lon"),
        ),
        check_vma=False,
    )
```
